32 devices in a mesh: seq: 8 (over y, x, core), tp: 4 (over z).
Axes of the slice: x: 2, y: 2, z: 4, core: 2. Of those that a mesh axis runs over, the one named last changes fastest.
Arguments:
- hidden_in: bfloat16 [2048, 4096], P('seq', 'tp'), may hold values from -6 to 6
- order: int32 [2048], P('seq'), may hold values from 0 to 2047, as said below
- segment: int32 [2048], replicated, may hold values from 0 to 3, never falling along the last dimension, each value on 1 to 1024 neighbouring positions
- norm_gain: float32 [4096], replicated, may hold values from 0.1 to 1.9
- w_query: bfloat16 [4096, 2048], P('seq', 'tp')
- w_key: bfloat16 [4096, 512], P('seq', 'tp'), may hold values from -0.09375 to 0.09375
- w_value: bfloat16 [4096, 512], P('seq', 'tp'), may hold values from -0.09375 to 0.09375
- w_out: bfloat16 [2048, 4096], P('seq', 'tp'), may hold values from -0.5 to 0.5
Outputs:
- attn_out: bfloat16 [2048, 4096], P('seq', 'tp')
The draws below stay inside these ranges and needn't reach their ends.
Inputs may be any that keep to these rules, and one draw needn't show every extreme that they name: order holds every position once; it is made of runs of 64 consecutive positions, each starting at a multiple of 64 and stored in rows that start at a multiple of 64. `segment`: never falls along positions.
All inputs are finite; a program needn't handle non-finite values.
Results may differ from the reference program's by a relative error of at most 0.014.
The reference program's roundings to bfloat16 on the way (of `normed`, `weights` and `attention`) count: a program that leaves them out, or rounds other values in their place, can miss the bound.
Values may be sent and summed in bfloat16 or wider, within the bound.
A program may use at most 128 MiB of HBM per device.

```python
import math
import jax
import jax.numpy as jnp
import numpy as np
from jax import lax

D = 4096
HEADS = 16
KV_HEADS = 4
HD = 128
BLK = 64
TOKENS = 2048


def draw_order(key, part):
    blocks = TOKENS // BLK
    shuffled = jax.random.permutation(key, blocks).astype(jnp.int32)
    inside = jnp.arange(BLK, dtype=jnp.int32)
    return (shuffled[:, None] * BLK + inside[None, :]).reshape(-1).astype(jnp.int32)


def draw_w_query(key, part):
    base = jax.random.normal(key, (D, HEADS * HD), jnp.float32) * D ** (-0.5)
    return base.astype(jnp.bfloat16)


def level_of(rng, extent, pieces, low, high):
    factor_of, own = 1.0, jax.random.fold_in(rng, 6)
    for dim, blocks in pieces:
        heights = jnp.exp(jax.random.uniform(jax.random.fold_in(own, dim), (blocks,), jnp.float32, low / len(pieces), high / len(pieces)))
        factor_of = factor_of * jnp.repeat(heights, extent[dim] // blocks).reshape([-1 if axis == dim else 1 for axis in range(len(extent))])
    return factor_of


def length_profile(amount, total, bound, slope):
    portions = [(1 << 20) // math.isqrt(rank ** slope) + 1 for rank in range(2, amount + 1)]
    surplus, counts = total - bound - (amount - 1), [1] * (amount - 1)
    while surplus > 0:
        movable = [i for i in range(amount - 1) if counts[i] < bound]
        pool, left = sum([portions[i] for i in movable]), surplus
        for i in movable:
            addition = min(bound - counts[i], max(1, left * portions[i] // pool), surplus)
            counts[i] = counts[i] + addition
            surplus = surplus - addition
    return np.array([bound] + counts)


def uneven(rng, number_of, total, reach, lean):
    if number_of == 2:
        one = jax.random.randint(rng, (), max(1, total - reach), min(reach, total - 1) + 1)
        return jnp.stack([one, total - one])
    sizes = jnp.asarray(length_profile(number_of, total, reach, lean), jnp.int32)
    twos = (number_of - 1) // 2
    source_of, sink = sizes[1:1 + 2 * twos:2], sizes[2:2 + 2 * twos:2]
    room = jnp.minimum(source_of - 1, reach - sink)
    passed = jax.random.randint(jax.random.fold_in(rng, 1), (twos,), 0, 1 << 20) % (room + 1)
    sizes = sizes.at[1:1 + 2 * twos:2].set(source_of - passed).at[2:2 + 2 * twos:2].set(sink + passed)
    return sizes[jax.random.permutation(jax.random.fold_in(rng, 2), number_of)]


def gaussian(own_key, extent, scale, most, shards=(), kind=jnp.bfloat16):
    result = jax.random.normal(own_key, extent, jnp.float32) * scale
    if len(shards) > 0:
        result = level_of(own_key, extent, shards, -0.22, 0.18) * result
    return jnp.clip(result, min=-most, max=most).astype(kind)


def setup_inputs(seed: int = 0) -> dict:
    arg_keys = jax.random.split(jax.random.key(seed), 9)
    return {
        "hidden_in": gaussian(arg_keys[0], (TOKENS, D), 1.0, 6.0, ((0, 8), (1, 4))),
        "order": draw_order(jax.random.fold_in(arg_keys[8], 71), 0),
        "segment": jnp.searchsorted(jnp.cumsum(uneven(arg_keys[2], max(2, TOKENS // (8 * BLK)), TOKENS, min(32 * BLK, TOKENS // 2), 1)), jnp.arange(TOKENS), side="right").astype(jnp.int32),
        "norm_gain": jnp.clip(1.0 + 0.18 * jax.random.normal(arg_keys[3], (D,), jnp.float32), 0.1, 1.9),
        "w_query": draw_w_query(jax.random.fold_in(arg_keys[8], 71), 0),
        "w_key": gaussian(arg_keys[5], (D, KV_HEADS * HD), D ** -0.5, 0.09375, ((0, 8), (1, 4))),
        "w_value": gaussian(arg_keys[6], (D, KV_HEADS * HD), D ** -0.5, 0.09375, ((0, 8), (1, 4))),
        "w_out": gaussian(arg_keys[7], (HEADS * HD, D), (HEADS * HD // 16) ** -0.5, 0.5, ((0, 8), (1, 4))),
    }


THETA = 500000.0
EPS = 1e-05

def rotary(block, positions):
    head_dim = block.shape[-1]
    width = head_dim // 2
    frequency = THETA ** (-jnp.arange(width, dtype=jnp.float32) * 2.0 / head_dim)
    angle = positions.astype(jnp.float32)[:, None] * frequency[None, :]
    cosine = jnp.cos(angle)[:, None, :]
    sine = jnp.sin(angle)[:, None, :]
    first = block[..., :width]
    second = block[..., width:]
    return jnp.concatenate([first * cosine - second * sine, second * cosine + first * sine], axis=-1)

def reference(hidden_in, order, segment, norm_gain, w_query, w_key, w_value, w_out):
    wide = hidden_in.astype(jnp.float32)
    mean_square = lax.optimization_barrier(jnp.mean(wide * wide, axis=1, keepdims=True))
    normed = (wide * lax.rsqrt(mean_square + EPS) * norm_gain[None, :]).astype(jnp.bfloat16)
    query = jnp.dot(normed, w_query, preferred_element_type=jnp.float32).reshape(TOKENS, HEADS, HD)
    key = jnp.dot(normed, w_key, preferred_element_type=jnp.float32).reshape(TOKENS, KV_HEADS, HD)
    value = jnp.dot(normed, w_value, preferred_element_type=jnp.float32).reshape(TOKENS, KV_HEADS, HD)
    query = lax.optimization_barrier((rotary(query, order) * HD ** (-0.5)).astype(jnp.bfloat16))
    key = lax.optimization_barrier(rotary(key, order).astype(jnp.bfloat16))
    value = lax.optimization_barrier(value.astype(jnp.bfloat16))
    group = HEADS // KV_HEADS
    query_wide = query.astype(jnp.float32).reshape(TOKENS, KV_HEADS, group, HD)
    key_wide = key.astype(jnp.float32)
    value_wide = value.astype(jnp.float32)
    document = jnp.take(segment, order, axis=0)
    block_rows = min(256, TOKENS)

    def attend(index):
        start = (index * block_rows).astype(jnp.int32)
        rows_query = lax.dynamic_slice_in_dim(query_wide, start, block_rows, 0)
        rows_order = lax.dynamic_slice_in_dim(order, start, block_rows, 0)
        rows_document = lax.dynamic_slice_in_dim(document, start, block_rows, 0)
        scores = jnp.einsum('rkgd,ckd->rkgc', rows_query, key_wide)
        allowed = (order[None, :] <= rows_order[:, None]) & (document[None, :] == rows_document[:, None])
        scores = jnp.where(allowed[:, None, None, :], scores, -jnp.inf)
        top = lax.optimization_barrier(jnp.max(scores, axis=-1, keepdims=True))
        weights = jnp.exp(scores - top)
        total = lax.optimization_barrier(jnp.sum(weights, axis=-1))
        rounded = lax.optimization_barrier(weights.astype(jnp.bfloat16)).astype(jnp.float32)
        mixed = jnp.einsum('rkgc,ckd->rkgd', rounded, value_wide)
        return (mixed / total[..., None]).astype(jnp.bfloat16)
    blocks = lax.map(attend, jnp.arange(TOKENS // block_rows, dtype=jnp.int32))
    attention = blocks.reshape(TOKENS, HEADS * HD)
    return jnp.dot(attention, w_out, preferred_element_type=jnp.float32).astype(jnp.bfloat16)
```

```python
import functools

import numpy as np
import jax
import jax.numpy as jnp
from jax import lax
from jax.experimental import pallas as pl
from jax.experimental.pallas import tpu as pltpu
from jax.sharding import PartitionSpec as P

HD = 128
THETA = 500000.0
EPS = 1e-05
BIG = 3.0e38
MESH = pl.DeviceIdType.MESH


def flip(index, mask):
    bit = 1
    out = index
    while bit <= mask:
        if mask & bit:
            out = out + bit * (1 - 2 * ((index // bit) % 2))
        bit *= 2
    return out


class SeqGather:
    def __init__(self, buf, block, size, send, recv):
        self.buf, self.block, self.size, self.send, self.recv = buf, block, size, send, recv
        self.me = lax.axis_index("seq")
        high = []
        bit = 2
        while bit < size:
            high.append(bit)
            bit *= 2
        self.orders = (high + [1], high[::-1] + [1])

    def rows(self, j, half):
        part = self.block // 2
        start = pl.multiple_of(flip(self.me, j) * self.block + half * part, 16)
        return self.buf.at[pl.ds(start, part)]

    def copy(self, j, half, bit):
        k = self.orders[half].index(bit)
        view = self.rows(j, half)
        return pltpu.make_async_remote_copy(
            src_ref=view,
            dst_ref=view,
            send_sem=self.send.at[half, j, k],
            recv_sem=self.recv.at[half, j ^ bit],
            device_id={"seq": flip(self.me, bit)},
            device_id_type=MESH,
        )

    def last(self, j, half):
        found = -1
        for r, bit in enumerate(self.orders[half]):
            if j & bit:
                found = r
        return found

    def arrived(self, j, half):
        bit = self.orders[half][self.last(j, half)]
        view = self.rows(j, half)
        pltpu.make_async_remote_copy(
            src_ref=view,
            dst_ref=view,
            send_sem=self.send.at[half, j ^ bit, self.last(j, half)],
            recv_sem=self.recv.at[half, j],
            device_id={"seq": flip(self.me, bit)},
            device_id_type=MESH,
        ).wait_recv()

    def begin(self):
        count = len(self.orders[0])
        for k in range(count):
            for half in (0, 1):
                self.copy(0, half, self.orders[half][k]).start()

    def step(self, j, half):
        self.arrived(j, half)
        for bit in self.orders[half][self.last(j, half) + 1 :]:
            self.copy(j, half, bit).start()

    def steps(self):
        todo = [(self.last(j, half), j, half) for j in range(1, self.size) for half in (0, 1)]
        todo.sort(key=lambda item: (item[0], bin(item[1]).count("1"), item[1], item[2]))
        return [functools.partial(self.step, j, half) for _, j, half in todo]

    def finish(self):
        for half in (0, 1):
            for j in range(self.size):
                for bit in self.orders[half][self.last(j, half) + 1 :]:
                    self.copy(j, half, bit).wait_send()


class LineGather:
    def __init__(self, view, pieces, size, send, recv):
        self.view, self.pieces, self.size, self.send, self.recv = view, pieces, size, send, recv
        self.me = lax.axis_index("tp")

    def copy(self, owner, piece, way):
        view = self.view(owner, piece)
        to = self.me + 1 if way == 0 else self.me - 1
        return pltpu.make_async_remote_copy(
            src_ref=view,
            dst_ref=view,
            send_sem=self.send.at[way, owner, piece],
            recv_sem=self.recv.at[owner, piece],
            device_id={"tp": to},
            device_id_type=MESH,
        )

    def can(self, way):
        return self.me < self.size - 1 if way == 0 else self.me > 0

    def begin(self, piece):
        for way in (0, 1):

            @pl.when(self.can(way))
            def _():
                self.copy(self.me, piece, way).start()

    def step(self, k, piece, use=None):
        for way in (0, 1):
            owner = self.me - k if way == 0 else self.me + k
            here = owner >= 0 if way == 0 else owner < self.size
            source = 1 - way

            @pl.when(here)
            def _():
                view = self.view(owner, piece)
                pltpu.make_async_remote_copy(
                    src_ref=view,
                    dst_ref=view,
                    send_sem=self.send.at[way, owner, piece],
                    recv_sem=self.recv.at[owner, piece],
                    device_id={"tp": self.me - 1 if way == 0 else self.me + 1},
                    device_id_type=MESH,
                ).wait_recv()

                @pl.when(self.can(way))
                def _():
                    self.copy(owner, piece, way).start()

        if use is not None:
            for way in (0, 1):
                owner = self.me - k if way == 0 else self.me + k
                here = owner >= 0 if way == 0 else owner < self.size

                @pl.when(here)
                def _():
                    use(owner, piece)

    def finish(self):
        for piece in range(self.pieces):
            for way in (0, 1):
                for k in range(self.size):
                    owner = self.me - k if way == 0 else self.me + k
                    here = owner >= 0 if way == 0 else owner < self.size

                    @pl.when(here & self.can(way))
                    def _():
                        self.copy(owner, piece, way).wait_send()


def layer(
    seq,
    tp,
    hidden,
    order_col,
    order_row,
    segment,
    gain,
    frequency,
    w_query,
    w_key,
    w_value,
    w_out,
    out,
    x_all,
    normed,
    w_all,
    o_all,
    kv_all,
    ord_all,
    cap,
    att,
    squares,
    qkv,
    cosine,
    sine,
    local,
    x_send,
    x_recv,
    a_send,
    a_recv,
    w_send,
    w_recv,
    o_send,
    o_recv,
    k_send,
    k_recv,
    p_send,
    p_recv,
):
    me = lax.axis_index("seq")
    mine = lax.axis_index("tp")
    rows = hidden.shape[0]
    width = hidden.shape[1]
    depth = w_query.shape[0]
    q_cols = w_query.shape[1]
    k_cols = w_key.shape[1]
    o_depth = w_out.shape[0]
    tokens = kv_all.shape[0]
    heads = q_cols // HD
    groups = k_cols // HD
    group = heads // groups

    own_w = pl.ds(pl.multiple_of(me * depth, 16), depth)
    own_o = pl.ds(pl.multiple_of(me * o_depth, 16), o_depth)
    loads = [
        pltpu.make_async_copy(hidden, x_all.at[mine], local.at[0]),
        pltpu.make_async_copy(w_query, w_all.at[own_w, pl.ds(0, q_cols)], local.at[1]),
        pltpu.make_async_copy(w_key, w_all.at[own_w, pl.ds(q_cols, k_cols)], local.at[2]),
        pltpu.make_async_copy(w_value, w_all.at[own_w, pl.ds(q_cols + k_cols, k_cols)], local.at[3]),
        pltpu.make_async_copy(w_out, o_all.at[own_o], local.at[4]),
    ]
    for load in loads:
        load.start()

    barrier = pltpu.get_barrier_semaphore()
    for away in range(1, seq):
        pl.semaphore_signal(
            barrier, inc=1, device_id={"seq": (me + away) % seq}, device_id_type=MESH
        )

    for away in range(1, tp):
        pl.semaphore_signal(
            barrier, inc=1, device_id={"tp": (mine + away) % tp}, device_id_type=MESH
        )

    ord_all[me] = jnp.broadcast_to(order_row[...], ord_all.shape[1:])
    pl.semaphore_wait(barrier, seq + tp - 2)

    half_rows = rows // 2
    xs = LineGather(
        lambda owner, piece: x_all.at[owner, pl.ds(piece * half_rows, half_rows)],
        2, tp, x_send, x_recv,
    )
    ws = SeqGather(w_all, depth, seq, w_send, w_recv)
    os_ = SeqGather(o_all, o_depth, seq, o_send, o_recv)
    ks = SeqGather(kv_all, rows, seq, k_send, k_recv)
    piece_cols = q_cols // 2
    ats = LineGather(
        lambda owner, piece: att.at[
            :, pl.ds(pl.multiple_of(owner * q_cols + piece * piece_cols, HD), piece_cols)
        ],
        2, tp, a_send, a_recv,
    )

    loads[0].wait()
    xs.begin(0)
    xs.begin(1)
    for load in loads[1:4]:
        load.wait()
    ws.begin()

    def positions(away):
        to = (me + away) % seq
        return pltpu.make_async_remote_copy(
            src_ref=ord_all.at[me],
            dst_ref=ord_all.at[me],
            send_sem=p_send.at[away],
            recv_sem=p_recv.at[away],
            device_id={"seq": to},
            device_id_type=MESH,
        )

    for away in range(1, seq):
        positions(away).start()
    loads[4].wait()

    def add_squares(owner, piece):
        where = pl.ds(piece * half_rows, half_rows)
        wide = x_all[owner, where].astype(jnp.float32)
        squares[where] += jnp.sum(wide * wide, axis=1, keepdims=True)

    squares[...] = jnp.zeros_like(squares)
    add_squares(mine, 0)
    add_squares(mine, 1)
    angle = order_col[...].astype(jnp.float32) * frequency[...]
    lane = lax.broadcasted_iota(jnp.int32, angle.shape, 1)
    cosine[...] = jnp.cos(angle)
    sine[...] = jnp.where(lane < HD // 2, -1.0, 1.0) * jnp.sin(angle)

    position = order_col[...]

    def find(block, total):
        at = pl.ds(pl.multiple_of(block * rows, HD), rows)
        index = lax.broadcasted_iota(jnp.int32, (rows, rows), 1) + block * rows
        number = jnp.broadcast_to(segment[:, at].astype(jnp.float32), (rows, rows))
        return total + jnp.sum(jnp.where(index == position, number, 0.0), axis=1, keepdims=True)

    document = lax.fori_loop(0, seq, find, jnp.zeros((rows, 1), jnp.float32))

    def before(block, total):
        at = pl.ds(pl.multiple_of(block * rows, HD), rows)
        number = jnp.broadcast_to(segment[:, at].astype(jnp.float32), (rows, rows))
        return total + jnp.sum(jnp.where(number < document, 1.0, 0.0), axis=1, keepdims=True)

    first = lax.fori_loop(0, seq, before, jnp.zeros((rows, 1), jnp.float32)).astype(jnp.int32)

    def masks():
        for away in range(1, seq):
            source = (me + seq - away) % seq
            pltpu.make_async_remote_copy(
                src_ref=ord_all.at[source],
                dst_ref=ord_all.at[source],
                send_sem=p_send.at[away],
                recv_sem=p_recv.at[away],
                device_id={"seq": source},
                device_id_type=MESH,
            ).wait_recv()

        def mask(block, carry):
            other = jnp.broadcast_to(ord_all[block][0:1], (rows, rows))
            allowed = (other <= position) & (other >= first)
            cap[:, pl.ds(pl.multiple_of(block * rows, HD), rows)] = jnp.where(allowed, BIG, -BIG)
            return carry

        lax.fori_loop(0, seq, mask, 0)

    line = [(k, piece) for k in range(1, tp) for piece in (0, 1)]
    steps = ws.steps()
    ring = [steps[: len(steps) * i // 6] for i in range(1, 7)]
    done = 0
    for i, (k, piece) in enumerate(line):
        if i < len(ring):
            last = i == len(ring) - 1
            for step in steps[done : len(ring[i])]:
                step()
            done = len(ring[i])
            if last:
                os_.begin()
        xs.step(k, piece, add_squares)
        if i == 0:
            masks()
    for step in steps[done:]:
        step()

    scale = lax.rsqrt(squares[...] * (1.0 / (tp * width)) + EPS)
    for t in range(tp):
        at = pl.ds(t * width, width)
        normed[:, at] = (x_all[t].astype(jnp.float32) * scale * gain[:, at]).astype(jnp.bfloat16)

    def rotate(block):
        return block * cosine[...] + pltpu.roll(block, HD // 2, 1) * sine[...]

    qkv[...] = jnp.dot(normed[...], w_all[...], preferred_element_type=jnp.float32)
    own_rows = pl.ds(pl.multiple_of(me * rows, 16), rows)
    for g in range(groups):
        key = qkv[:, pl.ds(q_cols + g * HD, HD)]
        kv_all[own_rows, pl.ds(g * HD, HD)] = rotate(key).astype(jnp.bfloat16)
        value = qkv[:, pl.ds(q_cols + k_cols + g * HD, HD)]
        kv_all[own_rows, pl.ds(k_cols + g * HD, HD)] = value.astype(jnp.bfloat16)
    ks.begin()
    queries = [
        (rotate(qkv[:, pl.ds(h * HD, HD)]) * HD ** (-0.5)).astype(jnp.bfloat16)
        for h in range(heads)
    ]
    for step in ks.steps():
        step()
    out_steps = os_.steps()
    early = [step for step in out_steps]

    chunk = min(tokens, 2048)
    chunks = tokens // chunk

    def part(h, start):
        g = h // group
        key = kv_all[pl.ds(start, chunk), pl.ds(g * HD, HD)]
        scores = lax.dot_general(
            queries[h], key, (((1,), (1,)), ((), ())), preferred_element_type=jnp.float32
        )
        return jnp.minimum(scores, cap[:, pl.ds(start, chunk)])

    def mix(h, start, weights):
        g = h // group
        value = kv_all[pl.ds(start, chunk), pl.ds(k_cols + g * HD, HD)]
        return jnp.dot(weights.astype(jnp.bfloat16), value, preferred_element_type=jnp.float32)

    per_piece = heads // 2
    for h in range(heads):
        scores = part(h, 0)
        top = jnp.max(scores, axis=1, keepdims=True)
        weights = jnp.exp(scores - top)
        total = jnp.sum(weights, axis=1, keepdims=True)
        weighted = mix(h, 0, weights)
        if chunks > 1:

            def more(block, state, h=h):
                top, total, weighted = state
                start = pl.multiple_of(block * chunk, HD)
                scores = part(h, start)
                higher = jnp.maximum(top, jnp.max(scores, axis=1, keepdims=True))
                shrink = jnp.exp(top - higher)
                weights = jnp.exp(scores - higher)
                total = total * shrink + jnp.sum(weights, axis=1, keepdims=True)
                return higher, total, weighted * shrink + mix(h, start, weights)

            top, total, weighted = lax.fori_loop(1, chunks, more, (top, total, weighted))
        at = pl.ds(pl.multiple_of(mine * q_cols + h * HD, HD), HD)
        att[:, at] = (weighted / total).astype(jnp.bfloat16)
        if (h + 1) % per_piece == 0:
            ats.begin((h + 1) // per_piece - 1)
        cut = [len(early) * i // heads for i in range(heads + 1)]
        for step in early[cut[h] : cut[h + 1]]:
            step()

    for k, piece in line:
        ats.step(k, piece)
    result = jnp.dot(att[...], o_all[...], preferred_element_type=jnp.float32)
    out[...] = result.astype(jnp.bfloat16)

    xs.finish()
    ats.finish()
    ws.finish()
    os_.finish()
    ks.finish()
    for away in range(1, seq):
        positions(away).wait_send()


def on_device(seq, tp, hidden_in, order, segment, norm_gain, w_query, w_key, w_value, w_out):
    rows, width = hidden_in.shape
    depth, q_cols = w_query.shape
    k_cols = w_key.shape[1]
    o_depth, o_cols = w_out.shape
    tokens = rows * seq
    half = np.float64(THETA) ** (-np.arange(HD // 2, dtype=np.float64) * 2.0 / HD)
    frequency = jnp.asarray(np.concatenate([half, half])[None, :].astype(np.float32))
    bits = max(1, (seq - 1).bit_length())
    dma = pltpu.SemaphoreType.DMA
    vmem = pl.BlockSpec(memory_space=pltpu.VMEM)
    away = pl.BlockSpec(memory_space=pl.ANY)
    flops = 2 * rows * (tp * width * (q_cols + 2 * k_cols) + tp * q_cols * o_cols)
    flops += 4 * rows * tokens * q_cols
    return pl.pallas_call(
        functools.partial(layer, seq, tp),
        out_shape=jax.ShapeDtypeStruct((rows, o_cols), jnp.bfloat16),
        in_specs=[away, vmem, vmem, vmem, vmem, vmem, away, away, away, away],
        out_specs=vmem,
        scratch_shapes=[
            pltpu.VMEM((tp, rows, width), jnp.bfloat16),
            pltpu.VMEM((rows, tp * width), jnp.bfloat16),
            pltpu.VMEM((seq * depth, q_cols + 2 * k_cols), jnp.bfloat16),
            pltpu.VMEM((seq * o_depth, o_cols), jnp.bfloat16),
            pltpu.VMEM((tokens, 2 * k_cols), jnp.bfloat16),
            pltpu.VMEM((seq, 8, rows), jnp.int32),
            pltpu.VMEM((rows, tokens), jnp.float32),
            pltpu.VMEM((rows, tp * q_cols), jnp.bfloat16),
            pltpu.VMEM((rows, 1), jnp.float32),
            pltpu.VMEM((rows, q_cols + 2 * k_cols), jnp.float32),
            pltpu.VMEM((rows, HD), jnp.float32),
            pltpu.VMEM((rows, HD), jnp.float32),
            dma((5,)),
            dma((2, tp, 2)),
            dma((tp, 2)),
            dma((2, tp, 2)),
            dma((tp, 2)),
            dma((2, seq, bits)),
            dma((2, seq)),
            dma((2, seq, bits)),
            dma((2, seq)),
            dma((2, seq, bits)),
            dma((2, seq)),
            dma((seq,)),
            dma((seq,)),
        ],
        compiler_params=pltpu.CompilerParams(
            collective_id=0, has_side_effects=True, vmem_limit_bytes=58 * 1024 * 1024
        ),
        cost_estimate=pl.CostEstimate(
            flops=flops, bytes_accessed=4 * 1024 * 1024, transcendentals=rows * tokens * q_cols // HD
        ),
    )(
        hidden_in,
        order.reshape(rows, 1),
        order.reshape(1, rows),
        segment.reshape(1, tokens),
        norm_gain.reshape(1, tp * width),
        frequency,
        w_query,
        w_key,
        w_value,
        w_out,
    )


def solution(mesh):
    placed = (
        P("seq", "tp"),
        P("seq"),
        P(),
        P(),
        P("seq", "tp"),
        P("seq", "tp"),
        P("seq", "tp"),
        P("seq", "tp"),
    )
    return jax.shard_map(
        functools.partial(on_device, mesh.shape["seq"], mesh.shape["tp"]),
        mesh=mesh,
        in_specs=placed,
        out_specs=P("seq", "tp"),
        check_vma=False,
    )
```

```python
import functools

import numpy as np
import jax
import jax.numpy as jnp
from jax import lax
from jax.experimental import pallas as pl
from jax.experimental.pallas import tpu as pltpu
from jax.sharding import PartitionSpec as P

HD = 128
THETA = 500000.0
EPS = 1e-05
BIG = 3.0e38
MESH = pl.DeviceIdType.MESH


def flip(index, mask):
    bit = 1
    out = index
    while bit <= mask:
        if mask & bit:
            out = out + bit * (1 - 2 * ((index // bit) % 2))
        bit *= 2
    return out


class SeqGather:
    def __init__(self, buf, block, size, send, recv):
        self.buf, self.block, self.size, self.send, self.recv = buf, block, size, send, recv
        self.me = lax.axis_index("seq")
        high = []
        bit = 2
        while bit < size:
            high.append(bit)
            bit *= 2
        self.orders = (high + [1], high[::-1] + [1])

    def rows(self, j, half):
        part = self.block // 2
        start = pl.multiple_of(flip(self.me, j) * self.block + half * part, 16)
        return self.buf.at[pl.ds(start, part)]

    def copy(self, j, half, bit):
        k = self.orders[half].index(bit)
        view = self.rows(j, half)
        return pltpu.make_async_remote_copy(
            src_ref=view,
            dst_ref=view,
            send_sem=self.send.at[half, j, k],
            recv_sem=self.recv.at[half, j ^ bit],
            device_id={"seq": flip(self.me, bit)},
            device_id_type=MESH,
        )

    def last(self, j, half):
        found = -1
        for r, bit in enumerate(self.orders[half]):
            if j & bit:
                found = r
        return found

    def arrived(self, j, half):
        bit = self.orders[half][self.last(j, half)]
        view = self.rows(j, half)
        pltpu.make_async_remote_copy(
            src_ref=view,
            dst_ref=view,
            send_sem=self.send.at[half, j ^ bit, self.last(j, half)],
            recv_sem=self.recv.at[half, j],
            device_id={"seq": flip(self.me, bit)},
            device_id_type=MESH,
        ).wait_recv()

    def begin(self):
        count = len(self.orders[0])
        for k in range(count):
            for half in (0, 1):
                self.copy(0, half, self.orders[half][k]).start()

    def step(self, j, half):
        self.arrived(j, half)
        for bit in self.orders[half][self.last(j, half) + 1 :]:
            self.copy(j, half, bit).start()

    def steps(self):
        todo = [(self.last(j, half), j, half) for j in range(1, self.size) for half in (0, 1)]
        todo.sort(key=lambda item: (item[0], bin(item[1]).count("1"), item[1], item[2]))
        return [functools.partial(self.step, j, half) for _, j, half in todo]

    def finish(self):
        for half in (0, 1):
            for j in range(self.size):
                for bit in self.orders[half][self.last(j, half) + 1 :]:
                    self.copy(j, half, bit).wait_send()


class LineGather:
    def __init__(self, view, pieces, size, send, recv):
        self.view, self.pieces, self.size, self.send, self.recv = view, pieces, size, send, recv
        self.me = lax.axis_index("tp")

    def copy(self, owner, piece, way):
        view = self.view(owner, piece)
        to = self.me + 1 if way == 0 else self.me - 1
        return pltpu.make_async_remote_copy(
            src_ref=view,
            dst_ref=view,
            send_sem=self.send.at[way, owner, piece],
            recv_sem=self.recv.at[owner, piece],
            device_id={"tp": to},
            device_id_type=MESH,
        )

    def can(self, way):
        return self.me < self.size - 1 if way == 0 else self.me > 0

    def begin(self, piece):
        for way in (0, 1):

            @pl.when(self.can(way))
            def _():
                self.copy(self.me, piece, way).start()

    def step(self, k, piece, use=None):
        for way in (0, 1):
            owner = self.me - k if way == 0 else self.me + k
            here = owner >= 0 if way == 0 else owner < self.size
            source = 1 - way

            @pl.when(here)
            def _():
                view = self.view(owner, piece)
                pltpu.make_async_remote_copy(
                    src_ref=view,
                    dst_ref=view,
                    send_sem=self.send.at[way, owner, piece],
                    recv_sem=self.recv.at[owner, piece],
                    device_id={"tp": self.me - 1 if way == 0 else self.me + 1},
                    device_id_type=MESH,
                ).wait_recv()

                @pl.when(self.can(way))
                def _():
                    self.copy(owner, piece, way).start()

        if use is not None:
            for way in (0, 1):
                owner = self.me - k if way == 0 else self.me + k
                here = owner >= 0 if way == 0 else owner < self.size

                @pl.when(here)
                def _():
                    use(owner, piece)

    def finish(self):
        for piece in range(self.pieces):
            for way in (0, 1):
                for k in range(self.size):
                    owner = self.me - k if way == 0 else self.me + k
                    here = owner >= 0 if way == 0 else owner < self.size

                    @pl.when(here & self.can(way))
                    def _():
                        self.copy(owner, piece, way).wait_send()


def layer(
    seq,
    tp,
    hidden,
    order_col,
    order_row,
    segment,
    gain,
    frequency,
    w_query,
    w_key,
    w_value,
    w_out,
    out,
    x_all,
    normed,
    w_all,
    o_all,
    kv_all,
    ord_all,
    cap,
    att,
    squares,
    qkv,
    cosine,
    sine,
    local,
    x_send,
    x_recv,
    a_send,
    a_recv,
    w_send,
    w_recv,
    o_send,
    o_recv,
    k_send,
    k_recv,
    p_send,
    p_recv,
):
    me = lax.axis_index("seq")
    mine = lax.axis_index("tp")
    rows = hidden.shape[0]
    width = hidden.shape[1]
    depth = w_query.shape[0]
    q_cols = w_query.shape[1]
    k_cols = w_key.shape[1]
    o_depth = w_out.shape[0]
    tokens = kv_all.shape[0]
    heads = q_cols // HD
    groups = k_cols // HD
    group = heads // groups

    own_w = pl.ds(pl.multiple_of(me * depth, 16), depth)
    own_o = pl.ds(pl.multiple_of(me * o_depth, 16), o_depth)
    loads = [
        pltpu.make_async_copy(hidden, x_all.at[mine], local.at[0]),
        pltpu.make_async_copy(w_query, w_all.at[own_w, pl.ds(0, q_cols)], local.at[1]),
        pltpu.make_async_copy(w_key, w_all.at[own_w, pl.ds(q_cols, k_cols)], local.at[2]),
        pltpu.make_async_copy(w_value, w_all.at[own_w, pl.ds(q_cols + k_cols, k_cols)], local.at[3]),
        pltpu.make_async_copy(w_out, o_all.at[own_o], local.at[4]),
    ]
    for load in loads:
        load.start()

    barrier = pltpu.get_barrier_semaphore()
    for away in range(1, seq):
        pl.semaphore_signal(
            barrier, inc=1, device_id={"seq": (me + away) % seq}, device_id_type=MESH
        )

    for away in range(1, tp):
        pl.semaphore_signal(
            barrier, inc=1, device_id={"tp": (mine + away) % tp}, device_id_type=MESH
        )

    ord_all[me] = jnp.broadcast_to(order_row[...], ord_all.shape[1:])
    pl.semaphore_wait(barrier, seq + tp - 2)

    half_rows = rows // 2
    xs = LineGather(
        lambda owner, piece: x_all.at[owner, pl.ds(piece * half_rows, half_rows)],
        2, tp, x_send, x_recv,
    )
    ws = SeqGather(w_all, depth, seq, w_send, w_recv)
    os_ = SeqGather(o_all, o_depth, seq, o_send, o_recv)
    ks = SeqGather(kv_all, rows, seq, k_send, k_recv)
    piece_cols = q_cols // heads
    ats = LineGather(
        lambda owner, piece: att.at[
            :, pl.ds(pl.multiple_of(owner * q_cols + piece * piece_cols, HD), piece_cols)
        ],
        heads, tp, a_send, a_recv,
    )

    loads[0].wait()
    xs.begin(0)
    xs.begin(1)
    for load in loads[1:4]:
        load.wait()
    ws.begin()

    def positions(away):
        to = (me + away) % seq
        return pltpu.make_async_remote_copy(
            src_ref=ord_all.at[me],
            dst_ref=ord_all.at[me],
            send_sem=p_send.at[away],
            recv_sem=p_recv.at[away],
            device_id={"seq": to},
            device_id_type=MESH,
        )

    for away in range(1, seq):
        positions(away).start()
    loads[4].wait()

    def add_squares(owner, piece):
        where = pl.ds(piece * half_rows, half_rows)
        wide = x_all[owner, where].astype(jnp.float32)
        squares[where] += jnp.sum(wide * wide, axis=1, keepdims=True)

    squares[...] = jnp.zeros_like(squares)
    add_squares(mine, 0)
    add_squares(mine, 1)
    angle = order_col[...].astype(jnp.float32) * frequency[...]
    lane = lax.broadcasted_iota(jnp.int32, angle.shape, 1)
    cosine[...] = jnp.cos(angle)
    sine[...] = jnp.where(lane < HD // 2, -1.0, 1.0) * jnp.sin(angle)

    position = order_col[...]

    def find(block, total):
        at = pl.ds(pl.multiple_of(block * rows, HD), rows)
        index = lax.broadcasted_iota(jnp.int32, (rows, rows), 1) + block * rows
        number = jnp.broadcast_to(segment[:, at].astype(jnp.float32), (rows, rows))
        return total + jnp.sum(jnp.where(index == position, number, 0.0), axis=1, keepdims=True)

    document = lax.fori_loop(0, seq, find, jnp.zeros((rows, 1), jnp.float32))

    def before(block, total):
        at = pl.ds(pl.multiple_of(block * rows, HD), rows)
        number = jnp.broadcast_to(segment[:, at].astype(jnp.float32), (rows, rows))
        return total + jnp.sum(jnp.where(number < document, 1.0, 0.0), axis=1, keepdims=True)

    first = lax.fori_loop(0, seq, before, jnp.zeros((rows, 1), jnp.float32)).astype(jnp.int32)

    def masks():
        for away in range(1, seq):
            source = (me + seq - away) % seq
            pltpu.make_async_remote_copy(
                src_ref=ord_all.at[source],
                dst_ref=ord_all.at[source],
                send_sem=p_send.at[away],
                recv_sem=p_recv.at[away],
                device_id={"seq": source},
                device_id_type=MESH,
            ).wait_recv()

        def mask(block, carry):
            other = jnp.broadcast_to(ord_all[block][0:1], (rows, rows))
            allowed = (other <= position) & (other >= first)
            cap[:, pl.ds(pl.multiple_of(block * rows, HD), rows)] = jnp.where(allowed, BIG, -BIG)
            return carry

        lax.fori_loop(0, seq, mask, 0)

    line = [(k, piece) for k in range(1, tp) for piece in (0, 1)]
    steps = ws.steps()
    ring = [steps[: len(steps) * i // 6] for i in range(1, 7)]
    done = 0
    for i, (k, piece) in enumerate(line):
        if i < len(ring):
            last = i == len(ring) - 1
            for step in steps[done : len(ring[i])]:
                step()
            done = len(ring[i])
            if last:
                os_.begin()
        xs.step(k, piece, add_squares)
        if i == 0:
            masks()
    for step in steps[done:]:
        step()

    scale = lax.rsqrt(squares[...] * (1.0 / (tp * width)) + EPS)
    for t in range(tp):
        at = pl.ds(t * width, width)
        normed[:, at] = (x_all[t].astype(jnp.float32) * scale * gain[:, at]).astype(jnp.bfloat16)

    def rotate(block):
        return block * cosine[...] + pltpu.roll(block, HD // 2, 1) * sine[...]

    qkv[...] = jnp.dot(normed[...], w_all[...], preferred_element_type=jnp.float32)
    own_rows = pl.ds(pl.multiple_of(me * rows, 16), rows)
    for g in range(groups):
        key = qkv[:, pl.ds(q_cols + g * HD, HD)]
        kv_all[own_rows, pl.ds(g * HD, HD)] = rotate(key).astype(jnp.bfloat16)
        value = qkv[:, pl.ds(q_cols + k_cols + g * HD, HD)]
        kv_all[own_rows, pl.ds(k_cols + g * HD, HD)] = value.astype(jnp.bfloat16)
    ks.begin()
    queries = [
        (rotate(qkv[:, pl.ds(h * HD, HD)]) * HD ** (-0.5)).astype(jnp.bfloat16)
        for h in range(heads)
    ]
    for step in ks.steps():
        step()
    out_steps = os_.steps()
    early = [step for step in out_steps]

    chunk = min(tokens, 2048)
    chunks = tokens // chunk

    def part(h, start):
        g = h // group
        key = kv_all[pl.ds(start, chunk), pl.ds(g * HD, HD)]
        scores = lax.dot_general(
            queries[h], key, (((1,), (1,)), ((), ())), preferred_element_type=jnp.float32
        )
        return jnp.minimum(scores, cap[:, pl.ds(start, chunk)])

    def mix(h, start, weights):
        g = h // group
        value = kv_all[pl.ds(start, chunk), pl.ds(k_cols + g * HD, HD)]
        return jnp.dot(weights.astype(jnp.bfloat16), value, preferred_element_type=jnp.float32)

    per_piece = 1
    for h in range(heads):
        scores = part(h, 0)
        top = jnp.max(scores, axis=1, keepdims=True)
        weights = jnp.exp(scores - top)
        total = jnp.sum(weights, axis=1, keepdims=True)
        weighted = mix(h, 0, weights)
        if chunks > 1:

            def more(block, state, h=h):
                top, total, weighted = state
                start = pl.multiple_of(block * chunk, HD)
                scores = part(h, start)
                higher = jnp.maximum(top, jnp.max(scores, axis=1, keepdims=True))
                shrink = jnp.exp(top - higher)
                weights = jnp.exp(scores - higher)
                total = total * shrink + jnp.sum(weights, axis=1, keepdims=True)
                return higher, total, weighted * shrink + mix(h, start, weights)

            top, total, weighted = lax.fori_loop(1, chunks, more, (top, total, weighted))
        at = pl.ds(pl.multiple_of(mine * q_cols + h * HD, HD), HD)
        att[:, at] = (weighted / total).astype(jnp.bfloat16)
        if (h + 1) % per_piece == 0:
            ats.begin((h + 1) // per_piece - 1)
        cut = [len(early) * i // heads for i in range(heads + 1)]
        for step in early[cut[h] : cut[h + 1]]:
            step()

    for k in range(1, tp):
        for piece in range(heads):
            ats.step(k, piece)
    result = jnp.dot(att[...], o_all[...], preferred_element_type=jnp.float32)
    out[...] = result.astype(jnp.bfloat16)

    xs.finish()
    ats.finish()
    ws.finish()
    os_.finish()
    ks.finish()
    for away in range(1, seq):
        positions(away).wait_send()


def on_device(seq, tp, hidden_in, order, segment, norm_gain, w_query, w_key, w_value, w_out):
    rows, width = hidden_in.shape
    depth, q_cols = w_query.shape
    k_cols = w_key.shape[1]
    o_depth, o_cols = w_out.shape
    tokens = rows * seq
    half = np.float64(THETA) ** (-np.arange(HD // 2, dtype=np.float64) * 2.0 / HD)
    frequency = jnp.asarray(np.concatenate([half, half])[None, :].astype(np.float32))
    bits = max(1, (seq - 1).bit_length())
    dma = pltpu.SemaphoreType.DMA
    vmem = pl.BlockSpec(memory_space=pltpu.VMEM)
    away = pl.BlockSpec(memory_space=pl.ANY)
    flops = 2 * rows * (tp * width * (q_cols + 2 * k_cols) + tp * q_cols * o_cols)
    flops += 4 * rows * tokens * q_cols
    return pl.pallas_call(
        functools.partial(layer, seq, tp),
        out_shape=jax.ShapeDtypeStruct((rows, o_cols), jnp.bfloat16),
        in_specs=[away, vmem, vmem, vmem, vmem, vmem, away, away, away, away],
        out_specs=vmem,
        scratch_shapes=[
            pltpu.VMEM((tp, rows, width), jnp.bfloat16),
            pltpu.VMEM((rows, tp * width), jnp.bfloat16),
            pltpu.VMEM((seq * depth, q_cols + 2 * k_cols), jnp.bfloat16),
            pltpu.VMEM((seq * o_depth, o_cols), jnp.bfloat16),
            pltpu.VMEM((tokens, 2 * k_cols), jnp.bfloat16),
            pltpu.VMEM((seq, 8, rows), jnp.int32),
            pltpu.VMEM((rows, tokens), jnp.float32),
            pltpu.VMEM((rows, tp * q_cols), jnp.bfloat16),
            pltpu.VMEM((rows, 1), jnp.float32),
            pltpu.VMEM((rows, q_cols + 2 * k_cols), jnp.float32),
            pltpu.VMEM((rows, HD), jnp.float32),
            pltpu.VMEM((rows, HD), jnp.float32),
            dma((5,)),
            dma((2, tp, 2)),
            dma((tp, 2)),
            dma((2, tp, q_cols // HD)),
            dma((tp, q_cols // HD)),
            dma((2, seq, bits)),
            dma((2, seq)),
            dma((2, seq, bits)),
            dma((2, seq)),
            dma((2, seq, bits)),
            dma((2, seq)),
            dma((seq,)),
            dma((seq,)),
        ],
        compiler_params=pltpu.CompilerParams(
            collective_id=0, has_side_effects=True, vmem_limit_bytes=58 * 1024 * 1024
        ),
        cost_estimate=pl.CostEstimate(
            flops=flops, bytes_accessed=4 * 1024 * 1024, transcendentals=rows * tokens * q_cols // HD
        ),
    )(
        hidden_in,
        order.reshape(rows, 1),
        order.reshape(1, rows),
        segment.reshape(1, tokens),
        norm_gain.reshape(1, tp * width),
        frequency,
        w_query,
        w_key,
        w_value,
        w_out,
    )


def solution(mesh):
    placed = (
        P("seq", "tp"),
        P("seq"),
        P(),
        P(),
        P("seq", "tp"),
        P("seq", "tp"),
        P("seq", "tp"),
        P("seq", "tp"),
    )
    return jax.shard_map(
        functools.partial(on_device, mesh.shape["seq"], mesh.shape["tp"]),
        mesh=mesh,
        in_specs=placed,
        out_specs=P("seq", "tp"),
        check_vma=False,
    )
```

```python
import functools

import numpy as np
import jax
import jax.numpy as jnp
from jax import lax
from jax.experimental import pallas as pl
from jax.experimental.pallas import tpu as pltpu
from jax.sharding import PartitionSpec as P

HD = 128
THETA = 500000.0
EPS = 1e-05
BIG = 3.0e38
MESH = pl.DeviceIdType.MESH


def flip(index, mask):
    bit = 1
    out = index
    while bit <= mask:
        if mask & bit:
            out = out + bit * (1 - 2 * ((index // bit) % 2))
        bit *= 2
    return out


class SeqGather:
    def __init__(self, buf, block, size, send, recv):
        self.buf, self.block, self.size, self.send, self.recv = buf, block, size, send, recv
        self.me = lax.axis_index("seq")
        high = []
        bit = 2
        while bit < size:
            high.append(bit)
            bit *= 2
        self.orders = (high + [1], high[::-1] + [1])

    def rows(self, j, half):
        part = self.block // 2
        start = pl.multiple_of(flip(self.me, j) * self.block + half * part, 16)
        return self.buf.at[pl.ds(start, part)]

    def copy(self, j, half, bit):
        k = self.orders[half].index(bit)
        view = self.rows(j, half)
        return pltpu.make_async_remote_copy(
            src_ref=view,
            dst_ref=view,
            send_sem=self.send.at[half, j, k],
            recv_sem=self.recv.at[half, j ^ bit],
            device_id={"seq": flip(self.me, bit)},
            device_id_type=MESH,
        )

    def last(self, j, half):
        found = -1
        for r, bit in enumerate(self.orders[half]):
            if j & bit:
                found = r
        return found

    def arrived(self, j, half):
        bit = self.orders[half][self.last(j, half)]
        view = self.rows(j, half)
        pltpu.make_async_remote_copy(
            src_ref=view,
            dst_ref=view,
            send_sem=self.send.at[half, j ^ bit, self.last(j, half)],
            recv_sem=self.recv.at[half, j],
            device_id={"seq": flip(self.me, bit)},
            device_id_type=MESH,
        ).wait_recv()

    def begin(self):
        count = len(self.orders[0])
        for k in range(count):
            for half in (0, 1):
                self.copy(0, half, self.orders[half][k]).start()

    def step(self, j, half):
        self.arrived(j, half)
        for bit in self.orders[half][self.last(j, half) + 1 :]:
            self.copy(j, half, bit).start()

    def steps(self):
        todo = [(self.last(j, half), j, half) for j in range(1, self.size) for half in (0, 1)]
        todo.sort(key=lambda item: (item[0], bin(item[1]).count("1"), item[1], item[2]))
        return [functools.partial(self.step, j, half) for _, j, half in todo]

    def finish(self):
        for half in (0, 1):
            for j in range(self.size):
                for bit in self.orders[half][self.last(j, half) + 1 :]:
                    self.copy(j, half, bit).wait_send()


class LineGather:
    def __init__(self, view, pieces, size, send, recv):
        self.view, self.pieces, self.size, self.send, self.recv = view, pieces, size, send, recv
        self.me = lax.axis_index("tp")

    def copy(self, owner, piece, way):
        view = self.view(owner, piece)
        to = self.me + 1 if way == 0 else self.me - 1
        return pltpu.make_async_remote_copy(
            src_ref=view,
            dst_ref=view,
            send_sem=self.send.at[way, owner, piece],
            recv_sem=self.recv.at[owner, piece],
            device_id={"tp": to},
            device_id_type=MESH,
        )

    def can(self, way):
        return self.me < self.size - 1 if way == 0 else self.me > 0

    def begin(self, piece):
        for way in (0, 1):

            @pl.when(self.can(way))
            def _():
                self.copy(self.me, piece, way).start()

    def step(self, k, piece, use=None):
        for way in (0, 1):
            owner = self.me - k if way == 0 else self.me + k
            here = owner >= 0 if way == 0 else owner < self.size
            source = 1 - way

            @pl.when(here)
            def _():
                view = self.view(owner, piece)
                pltpu.make_async_remote_copy(
                    src_ref=view,
                    dst_ref=view,
                    send_sem=self.send.at[way, owner, piece],
                    recv_sem=self.recv.at[owner, piece],
                    device_id={"tp": self.me - 1 if way == 0 else self.me + 1},
                    device_id_type=MESH,
                ).wait_recv()

                @pl.when(self.can(way))
                def _():
                    self.copy(owner, piece, way).start()

        if use is not None:
            for way in (0, 1):
                owner = self.me - k if way == 0 else self.me + k
                here = owner >= 0 if way == 0 else owner < self.size

                @pl.when(here)
                def _():
                    use(owner, piece)

    def finish(self):
        for piece in range(self.pieces):
            for way in (0, 1):
                for k in range(self.size):
                    owner = self.me - k if way == 0 else self.me + k
                    here = owner >= 0 if way == 0 else owner < self.size

                    @pl.when(here & self.can(way))
                    def _():
                        self.copy(owner, piece, way).wait_send()


def layer(
    seq,
    tp,
    hidden,
    order_col,
    order_row,
    segment,
    gain,
    frequency,
    w_query,
    w_key,
    w_value,
    w_out,
    out,
    x_all,
    normed,
    w_all,
    o_all,
    kv_all,
    ord_all,
    cap,
    att,
    squares,
    qkv,
    cosine,
    sine,
    local,
    x_send,
    x_recv,
    a_send,
    a_recv,
    w_send,
    w_recv,
    o_send,
    o_recv,
    k_send,
    k_recv,
    p_send,
    p_recv,
):
    me = lax.axis_index("seq")
    mine = lax.axis_index("tp")
    rows = hidden.shape[0]
    width = hidden.shape[1]
    depth = w_query.shape[0]
    q_cols = w_query.shape[1]
    k_cols = w_key.shape[1]
    o_depth = w_out.shape[0]
    tokens = kv_all.shape[0]
    heads = q_cols // HD
    groups = k_cols // HD
    group = heads // groups

    own_w = pl.ds(pl.multiple_of(me * depth, 16), depth)
    own_o = pl.ds(pl.multiple_of(me * o_depth, 16), o_depth)
    loads = [
        pltpu.make_async_copy(hidden, x_all.at[mine], local.at[0]),
        pltpu.make_async_copy(w_query, w_all.at[own_w, pl.ds(0, q_cols)], local.at[1]),
        pltpu.make_async_copy(w_key, w_all.at[own_w, pl.ds(q_cols, k_cols)], local.at[2]),
        pltpu.make_async_copy(w_value, w_all.at[own_w, pl.ds(q_cols + k_cols, k_cols)], local.at[3]),
        pltpu.make_async_copy(w_out, o_all.at[own_o], local.at[4]),
    ]
    for load in loads:
        load.start()

    barrier = pltpu.get_barrier_semaphore()
    for away in range(1, seq):
        pl.semaphore_signal(
            barrier, inc=1, device_id={"seq": (me + away) % seq}, device_id_type=MESH
        )

    for away in range(1, tp):
        pl.semaphore_signal(
            barrier, inc=1, device_id={"tp": (mine + away) % tp}, device_id_type=MESH
        )

    ord_all[me] = jnp.broadcast_to(order_row[...], ord_all.shape[1:])
    pl.semaphore_wait(barrier, seq + tp - 2)

    half_rows = rows // 4
    xs = LineGather(
        lambda owner, piece: x_all.at[owner, pl.ds(piece * half_rows, half_rows)],
        4, tp, x_send, x_recv,
    )
    ws = SeqGather(w_all, depth, seq, w_send, w_recv)
    os_ = SeqGather(o_all, o_depth, seq, o_send, o_recv)
    ks = SeqGather(kv_all, rows, seq, k_send, k_recv)
    piece_cols = q_cols // heads
    ats = LineGather(
        lambda owner, piece: att.at[
            :, pl.ds(pl.multiple_of(owner * q_cols + piece * piece_cols, HD), piece_cols)
        ],
        heads, tp, a_send, a_recv,
    )

    loads[0].wait()
    for piece in range(4):
        xs.begin(piece)
    for load in loads[1:4]:
        load.wait()
    ws.begin()

    def positions(away):
        to = (me + away) % seq
        return pltpu.make_async_remote_copy(
            src_ref=ord_all.at[me],
            dst_ref=ord_all.at[me],
            send_sem=p_send.at[away],
            recv_sem=p_recv.at[away],
            device_id={"seq": to},
            device_id_type=MESH,
        )

    for away in range(1, seq):
        positions(away).start()
    loads[4].wait()

    def add_squares(owner, piece):
        where = pl.ds(piece * half_rows, half_rows)
        wide = x_all[owner, where].astype(jnp.float32)
        squares[where] += jnp.sum(wide * wide, axis=1, keepdims=True)

    squares[...] = jnp.zeros_like(squares)
    for piece in range(4):
        add_squares(mine, piece)
    angle = order_col[...].astype(jnp.float32) * frequency[...]
    lane = lax.broadcasted_iota(jnp.int32, angle.shape, 1)
    cosine[...] = jnp.cos(angle)
    sine[...] = jnp.where(lane < HD // 2, -1.0, 1.0) * jnp.sin(angle)

    position = order_col[...]

    def find(block, total):
        at = pl.ds(pl.multiple_of(block * rows, HD), rows)
        index = lax.broadcasted_iota(jnp.int32, (rows, rows), 1) + block * rows
        number = jnp.broadcast_to(segment[:, at].astype(jnp.float32), (rows, rows))
        return total + jnp.sum(jnp.where(index == position, number, 0.0), axis=1, keepdims=True)

    document = lax.fori_loop(0, seq, find, jnp.zeros((rows, 1), jnp.float32))

    def before(block, total):
        at = pl.ds(pl.multiple_of(block * rows, HD), rows)
        number = jnp.broadcast_to(segment[:, at].astype(jnp.float32), (rows, rows))
        return total + jnp.sum(jnp.where(number < document, 1.0, 0.0), axis=1, keepdims=True)

    first = lax.fori_loop(0, seq, before, jnp.zeros((rows, 1), jnp.float32)).astype(jnp.int32)

    def masks():
        for away in range(1, seq):
            source = (me + seq - away) % seq
            pltpu.make_async_remote_copy(
                src_ref=ord_all.at[source],
                dst_ref=ord_all.at[source],
                send_sem=p_send.at[away],
                recv_sem=p_recv.at[away],
                device_id={"seq": source},
                device_id_type=MESH,
            ).wait_recv()

        def mask(block, carry):
            other = jnp.broadcast_to(ord_all[block][0:1], (rows, rows))
            allowed = (other <= position) & (other >= first)
            cap[:, pl.ds(pl.multiple_of(block * rows, HD), rows)] = jnp.where(allowed, BIG, -BIG)
            return carry

        lax.fori_loop(0, seq, mask, 0)

    line = [(k, piece) for k in range(1, tp) for piece in range(4)]
    steps = ws.steps()
    ring = [steps[: len(steps) * i // len(line)] for i in range(1, len(line) + 1)]
    done = 0
    for i, (k, piece) in enumerate(line):
        if i < len(ring):
            last = i == len(ring) - 1
            for step in steps[done : len(ring[i])]:
                step()
            done = len(ring[i])
            if last:
                os_.begin()
        xs.step(k, piece, add_squares)
        if i == 0:
            masks()
    for step in steps[done:]:
        step()

    scale = lax.rsqrt(squares[...] * (1.0 / (tp * width)) + EPS)
    for t in range(tp):
        at = pl.ds(t * width, width)
        normed[:, at] = (x_all[t].astype(jnp.float32) * scale * gain[:, at]).astype(jnp.bfloat16)

    def rotate(block):
        return block * cosine[...] + pltpu.roll(block, HD // 2, 1) * sine[...]

    qkv[...] = jnp.dot(normed[...], w_all[...], preferred_element_type=jnp.float32)
    own_rows = pl.ds(pl.multiple_of(me * rows, 16), rows)
    for g in range(groups):
        key = qkv[:, pl.ds(q_cols + g * HD, HD)]
        kv_all[own_rows, pl.ds(g * HD, HD)] = rotate(key).astype(jnp.bfloat16)
        value = qkv[:, pl.ds(q_cols + k_cols + g * HD, HD)]
        kv_all[own_rows, pl.ds(k_cols + g * HD, HD)] = value.astype(jnp.bfloat16)
    ks.begin()
    queries = [
        (rotate(qkv[:, pl.ds(h * HD, HD)]) * HD ** (-0.5)).astype(jnp.bfloat16)
        for h in range(heads)
    ]
    for step in ks.steps():
        step()
    out_steps = os_.steps()
    early = [step for step in out_steps]

    chunk = min(tokens, 2048)
    chunks = tokens // chunk

    def part(h, start):
        g = h // group
        key = kv_all[pl.ds(start, chunk), pl.ds(g * HD, HD)]
        scores = lax.dot_general(
            queries[h], key, (((1,), (1,)), ((), ())), preferred_element_type=jnp.float32
        )
        return jnp.minimum(scores, cap[:, pl.ds(start, chunk)])

    def mix(h, start, weights):
        g = h // group
        value = kv_all[pl.ds(start, chunk), pl.ds(k_cols + g * HD, HD)]
        return jnp.dot(weights.astype(jnp.bfloat16), value, preferred_element_type=jnp.float32)

    per_piece = 1
    for h in range(heads):
        scores = part(h, 0)
        top = jnp.max(scores, axis=1, keepdims=True)
        weights = jnp.exp(scores - top)
        total = jnp.sum(weights, axis=1, keepdims=True)
        weighted = mix(h, 0, weights)
        if chunks > 1:

            def more(block, state, h=h):
                top, total, weighted = state
                start = pl.multiple_of(block * chunk, HD)
                scores = part(h, start)
                higher = jnp.maximum(top, jnp.max(scores, axis=1, keepdims=True))
                shrink = jnp.exp(top - higher)
                weights = jnp.exp(scores - higher)
                total = total * shrink + jnp.sum(weights, axis=1, keepdims=True)
                return higher, total, weighted * shrink + mix(h, start, weights)

            top, total, weighted = lax.fori_loop(1, chunks, more, (top, total, weighted))
        at = pl.ds(pl.multiple_of(mine * q_cols + h * HD, HD), HD)
        att[:, at] = (weighted / total).astype(jnp.bfloat16)
        if (h + 1) % per_piece == 0:
            ats.begin((h + 1) // per_piece - 1)
        cut = [len(early) * i // heads for i in range(heads + 1)]
        for step in early[cut[h] : cut[h + 1]]:
            step()

    for k in range(1, tp):
        for piece in range(heads):
            ats.step(k, piece)
    result = jnp.dot(att[...], o_all[...], preferred_element_type=jnp.float32)
    out[...] = result.astype(jnp.bfloat16)

    xs.finish()
    ats.finish()
    ws.finish()
    os_.finish()
    ks.finish()
    for away in range(1, seq):
        positions(away).wait_send()


def on_device(seq, tp, hidden_in, order, segment, norm_gain, w_query, w_key, w_value, w_out):
    rows, width = hidden_in.shape
    depth, q_cols = w_query.shape
    k_cols = w_key.shape[1]
    o_depth, o_cols = w_out.shape
    tokens = rows * seq
    half = np.float64(THETA) ** (-np.arange(HD // 2, dtype=np.float64) * 2.0 / HD)
    frequency = jnp.asarray(np.concatenate([half, half])[None, :].astype(np.float32))
    bits = max(1, (seq - 1).bit_length())
    dma = pltpu.SemaphoreType.DMA
    vmem = pl.BlockSpec(memory_space=pltpu.VMEM)
    away = pl.BlockSpec(memory_space=pl.ANY)
    flops = 2 * rows * (tp * width * (q_cols + 2 * k_cols) + tp * q_cols * o_cols)
    flops += 4 * rows * tokens * q_cols
    return pl.pallas_call(
        functools.partial(layer, seq, tp),
        out_shape=jax.ShapeDtypeStruct((rows, o_cols), jnp.bfloat16),
        in_specs=[away, vmem, vmem, vmem, vmem, vmem, away, away, away, away],
        out_specs=vmem,
        scratch_shapes=[
            pltpu.VMEM((tp, rows, width), jnp.bfloat16),
            pltpu.VMEM((rows, tp * width), jnp.bfloat16),
            pltpu.VMEM((seq * depth, q_cols + 2 * k_cols), jnp.bfloat16),
            pltpu.VMEM((seq * o_depth, o_cols), jnp.bfloat16),
            pltpu.VMEM((tokens, 2 * k_cols), jnp.bfloat16),
            pltpu.VMEM((seq, 8, rows), jnp.int32),
            pltpu.VMEM((rows, tokens), jnp.float32),
            pltpu.VMEM((rows, tp * q_cols), jnp.bfloat16),
            pltpu.VMEM((rows, 1), jnp.float32),
            pltpu.VMEM((rows, q_cols + 2 * k_cols), jnp.float32),
            pltpu.VMEM((rows, HD), jnp.float32),
            pltpu.VMEM((rows, HD), jnp.float32),
            dma((5,)),
            dma((2, tp, 4)),
            dma((tp, 4)),
            dma((2, tp, q_cols // HD)),
            dma((tp, q_cols // HD)),
            dma((2, seq, bits)),
            dma((2, seq)),
            dma((2, seq, bits)),
            dma((2, seq)),
            dma((2, seq, bits)),
            dma((2, seq)),
            dma((seq,)),
            dma((seq,)),
        ],
        compiler_params=pltpu.CompilerParams(
            collective_id=0, has_side_effects=True, vmem_limit_bytes=58 * 1024 * 1024
        ),
        cost_estimate=pl.CostEstimate(
            flops=flops, bytes_accessed=4 * 1024 * 1024, transcendentals=rows * tokens * q_cols // HD
        ),
    )(
        hidden_in,
        order.reshape(rows, 1),
        order.reshape(1, rows),
        segment.reshape(1, tokens),
        norm_gain.reshape(1, tp * width),
        frequency,
        w_query,
        w_key,
        w_value,
        w_out,
    )


def solution(mesh):
    placed = (
        P("seq", "tp"),
        P("seq"),
        P(),
        P(),
        P("seq", "tp"),
        P("seq", "tp"),
        P("seq", "tp"),
        P("seq", "tp"),
    )
    return jax.shard_map(
        functools.partial(on_device, mesh.shape["seq"], mesh.shape["tp"]),
        mesh=mesh,
        in_specs=placed,
        out_specs=P("seq", "tp"),
        check_vma=False,
    )
```
